32 devices in a mesh: wide: 8 (over z, x), narrow: 4 (over y, core).
Axes of the slice: x: 2, y: 2, z: 4, core: 2. Of those that a mesh axis runs over, the one named last changes fastest.
Arguments:
- amplitudes: float32 [240, 72000], P('narrow', 'wide'), may hold values from -6 to 6
- integrals: float32 [72000, 1920], P('wide', 'narrow'), may hold values from -0.0234375 to 0.0234375
- occupied_energy: float32 [60], replicated, may hold values from -3 to -1
- virtual_energy_rows: float32 [4], replicated, may hold values from 0.2 to 1.2
- virtual_energy_cols: float32 [32], replicated, may hold values from 0.2 to 1.2
Outputs:
- amplitude_step: float32 [240, 1920], P('wide', 'narrow')
The draws below stay inside these ranges and needn't reach their ends.
All inputs are finite; a program needn't handle non-finite values.
Results may differ from the reference program's by a relative error of at most 0.00012.
Values sent between devices are 32-bit elements; how exact they have to be, the bound alone decides.
A program may use at most 64 MiB of HBM per device.

```python
import jax
import jax.numpy as jnp
from jax import lax

O = 60
AB = 4
BB = 32
KPAIRS = 72000
ROWS = 240
COLS = 1920


def block_scale(own_key, extent, pieces, smallest, top_value):
    def one(dim, blocks):
        draws = jax.random.uniform(jax.random.fold_in(jax.random.fold_in(own_key, 6), dim), (blocks,), jnp.float32, smallest / len(pieces), top_value / len(pieces))
        return jnp.repeat(jnp.exp(draws), extent[dim] // blocks).reshape((-1,) + (1,) * (len(extent) - dim - 1))

    loudness = one(*pieces[0])
    for cut in pieces[1:]:
        loudness = loudness * one(*cut)
    return loudness


def centred(key, dims, scale, bound, pieces=(), held_as=jnp.bfloat16):
    values = scale * jax.random.normal(key, dims, jnp.float32)
    if pieces:
        values = values * block_scale(key, dims, pieces, -0.22, 0.18)
    return jnp.clip(values, -bound, bound).astype(held_as)


def setup_inputs(seed: int = 0) -> dict:
    arg_keys = jax.random.split(jax.random.key(seed), 6)
    return {
        "amplitudes": centred(arg_keys[0], (ROWS, KPAIRS), 1.0, 6.0, ((0, 4), (1, 8)), jnp.float32),
        "integrals": centred(arg_keys[1], (KPAIRS, COLS), KPAIRS ** -0.5, 0.0234375, ((0, 8), (1, 4)), jnp.float32),
        "occupied_energy": jnp.clip(jax.random.uniform(arg_keys[2], (O,), jnp.float32, -3.0, -1.0), -3.0, -1.0),
        "virtual_energy_rows": jnp.clip(jax.random.uniform(arg_keys[3], (AB,), jnp.float32, 0.2, 1.2), 0.2, 1.2),
        "virtual_energy_cols": jnp.clip(jax.random.uniform(arg_keys[4], (BB,), jnp.float32, 0.2, 1.2), 0.2, 1.2),
    }


def reference(amplitudes, integrals, occupied_energy, virtual_energy_rows, virtual_energy_cols):
    cycle_term = jnp.dot(amplitudes, integrals, precision=lax.Precision.HIGHEST, preferred_element_type=jnp.float32)
    row_energy = (occupied_energy[None, :] - virtual_energy_rows[:, None]).reshape(-1)
    col_energy = (occupied_energy[None, :] - virtual_energy_cols[:, None]).reshape(-1)
    denominator = row_energy[:, None] + col_energy[None, :]
    return cycle_term / denominator
```

```python
import functools

import jax
import jax.numpy as jnp
from jax import lax
from jax.experimental import pallas as pl
from jax.experimental.pallas import tpu as pltpu
from jax.sharding import PartitionSpec as P

MESH = pl.DeviceIdType.MESH
F32 = jnp.float32
BF16 = jnp.bfloat16
DEPTH = 1152


def halves(values):
    high = values.astype(BF16)
    return high, (values - high.astype(F32)).astype(BF16)


def cycle_kernel(
    wides, amp, ints, out,
    own, mine, twin, far, far_twin, wide_ints, ints_high, ints_low,
    even, odd, group_sum, last_even, last_odd,
    send_big, send_small, recv_big, recv_small,
    own_sem, ints_sem, far_send, far_recv, pass_send, pass_recv, twin_send, twin_recv,
    sum_send, sum_recv,
):
    rows, pairs = amp.shape
    owner_rows = rows // 2
    third = 2 * owner_rows // 5
    small = owner_rows - 2 * third
    steps = mine.shape[0]
    slices = ints_high.shape[0]
    me = lax.axis_index("wide")
    narrow = lax.axis_index("narrow")
    across = lax.div(narrow, 2)
    core = lax.rem(narrow, 2)
    sibling = narrow + 1 - 2 * core
    neighbour = narrow + 2 - 4 * across
    diagonal = sibling + 2 - 4 * across
    shards = (narrow, sibling, neighbour, diagonal)

    own_copy = pltpu.make_async_copy(amp, own, own_sem)
    own_copy.start()

    def ints_copy(k, length):
        return pltpu.make_async_copy(
            ints.at[pl.ds(k * DEPTH, length)],
            wide_ints.at[k, pl.ds(0, length)],
            ints_sem.at[k],
        )

    last_length = pairs - (slices - 1) * DEPTH
    for k in range(slices):
        ints_copy(k, DEPTH if k < slices - 1 else last_length).start()
    if last_length < DEPTH:
        wide_ints[slices - 1, last_length:, :] = jnp.zeros(
            (DEPTH - last_length, ints.shape[1]), F32
        )

    barrier = pltpu.get_barrier_semaphore()
    for other in (sibling, neighbour):
        pl.semaphore_signal(barrier, inc=1, device_id=(me, other), device_id_type=MESH)
    for hop in range(1, wides):
        pl.semaphore_signal(
            barrier, inc=1, device_id=(lax.rem(me + hop, wides), narrow), device_id_type=MESH
        )
    pl.semaphore_wait(barrier, wides + 1)

    def far_copy(i):
        return pltpu.make_async_remote_copy(
            src_ref=mine.at[i], dst_ref=far.at[i],
            send_sem=far_send.at[i], recv_sem=far_recv.at[i],
            device_id=(me, neighbour), device_id_type=MESH,
        )

    def pass_copy(i):
        return pltpu.make_async_remote_copy(
            src_ref=far.at[i], dst_ref=far_twin.at[i],
            send_sem=pass_send.at[i], recv_sem=pass_recv.at[i],
            device_id=(me, sibling), device_id_type=MESH,
        )

    twin_copy = pltpu.make_async_remote_copy(
        src_ref=mine, dst_ref=twin, send_sem=twin_send, recv_sem=twin_recv,
        device_id=(me, sibling), device_id_type=MESH,
    )

    def pack(i, at, first, count, k):
        length = min(DEPTH, pairs - k * DEPTH)
        mine[i, at:at + count, :length] = own[first:first + count, k * DEPTH:k * DEPTH + length]
        if length < DEPTH:
            mine[i, at:at + count, length:] = jnp.zeros((count, DEPTH - length), F32)

    own_copy.wait()
    for g in range(2):
        for k in range(slices):
            i = g * slices + k
            pack(i, 0, g * third, third, k)
            pack(i, third, owner_rows + g * third, third, k)
            far_copy(i).start()
    for j in range(slices // 2):
        i = 2 * slices + j
        for p in range(2):
            pack(i, 2 * small * p, 2 * third, small, 2 * j + p)
            pack(i, 2 * small * p + small, owner_rows + 2 * third, small, 2 * j + p)
        far_copy(i).start()
    twin_copy.start()

    def sum_copy(s, h, g):
        owner = 2 * shards[s] + h
        src = send_big.at[s, h, g] if g < 2 else send_small.at[s, h]
        dst = recv_big.at[g, me] if g < 2 else recv_small.at[me]
        copy = pltpu.make_async_remote_copy(
            src_ref=src, dst_ref=dst,
            send_sem=sum_send.at[s, h, g], recv_sem=sum_recv.at[g, me],
            device_id=(owner, narrow), device_id_type=MESH,
        )
        return owner, copy

    def emit(s, h, g, value):
        if g < 2:
            send_big[s, h, g] = value
        else:
            send_small[s, h] = value
        owner, copy = sum_copy(s, h, g)

        @pl.when(owner == me)
        def _():
            if g < 2:
                recv_big[g, me] = value
            else:
                recv_small[me] = value

        @pl.when(owner != me)
        def _():
            copy.start()

    def product(values, k):
        high, low = halves(values)
        count = values.shape[0]
        both = jnp.dot(
            jnp.concatenate([high, low], axis=0), ints_high[k], preferred_element_type=F32
        )
        rest = jnp.dot(high, ints_low[k], preferred_element_type=F32)
        return both[:count] + (both[count:] + rest)

    even[...] = jnp.zeros_like(even)
    odd[...] = jnp.zeros_like(odd)
    twin_copy.wait_recv()

    def near_step(j, carry):
        for p, total in ((0, even), (1, odd)):
            k = 2 * j + p
            if p == 0 or last_length == DEPTH:
                ints_copy(k, DEPTH).wait()
            else:
                @pl.when(j < slices // 2 - 1)
                def _():
                    ints_copy(k, DEPTH).wait()

                @pl.when(j == slices // 2 - 1)
                def _():
                    ints_copy(slices - 1, last_length).wait()

            def split(t, inner):
                part = pl.ds(pl.multiple_of(t * 128, 128), 128)
                high, low = halves(wide_ints[k, part, :])
                ints_high[k, part, :] = high
                ints_low[k, part, :] = low
                return inner

            lax.fori_loop(0, DEPTH // 128, split, 0)
            blocks = [
                mine[k], mine[slices + k], twin[k], twin[slices + k],
                mine[2 * slices + j], twin[2 * slices + j],
            ]
            total[...] += product(jnp.concatenate(blocks, axis=0), k)
        return carry

    lax.fori_loop(0, slices // 2, near_step, 0)
    for s in range(2):
        for h in range(2):
            for g in range(2):
                at = 4 * third * s + 2 * third * g + third * h
                emit(s, h, g, even[at:at + third] + odd[at:at + third])
            at = 8 * third + 4 * small * s + small * h
            emit(s, h, 2, even[at:at + small] + odd[at + 2 * small:at + 3 * small])

    def arrive(i):
        far_copy(i).wait_recv()
        pass_copy(i).start()

    def far_block(i):
        pass_copy(i).wait_recv()
        return jnp.concatenate([far[i], far_twin[i]], axis=0)

    arrive(0)
    for g in range(2):
        group_sum[...] = jnp.zeros_like(group_sum)

        def far_step(k, carry):
            arrive(g * slices + k + 1)
            group_sum[...] += product(far_block(g * slices + k), k)
            return carry

        lax.fori_loop(0, slices, far_step, 0)
        for s in range(2):
            for h in range(2):
                at = 2 * third * s + third * h
                emit(2 + s, h, g, group_sum[at:at + third])

    last_even[...] = jnp.zeros_like(last_even)
    last_odd[...] = jnp.zeros_like(last_odd)

    def last_step(j, carry):
        @pl.when(j < slices // 2 - 1)
        def _():
            arrive(2 * slices + j + 1)

        block = far_block(2 * slices + j)
        last_even[...] += product(block, 2 * j)
        last_odd[...] += product(block, 2 * j + 1)
        return carry

    lax.fori_loop(0, slices // 2, last_step, 0)
    for s in range(2):
        for h in range(2):
            at = 4 * small * s + small * h
            emit(2 + s, h, 2, last_even[at:at + small] + last_odd[at + 2 * small:at + 3 * small])

    def drain(i, carry):
        far_copy(i).wait_send()
        pass_copy(i).wait_send()
        return carry

    lax.fori_loop(0, steps, drain, 0)
    twin_copy.wait_send()

    for g in range(3):
        for source in range(wides):
            @pl.when(me != source)
            def _():
                dst = recv_big.at[g, source] if g < 2 else recv_small.at[source]
                pltpu.make_async_remote_copy(
                    src_ref=dst, dst_ref=dst,
                    send_sem=sum_send.at[0, 0, g], recv_sem=sum_recv.at[g, source],
                    device_id=(source, narrow), device_id_type=MESH,
                ).wait_recv()
        held = recv_big.at[g] if g < 2 else recv_small
        total = held[0]
        for source in range(1, wides):
            total = total + held[source]
        out[g * third:g * third + total.shape[0], :] = total

    for s in range(4):
        for h in range(2):
            for g in range(3):
                owner, copy = sum_copy(s, h, g)

                @pl.when(owner != me)
                def _():
                    copy.wait_send()


def fused_term(amplitudes, integrals, wides):
    rows, pairs = amplitudes.shape
    cols = integrals.shape[1]
    owner_rows = rows // 2
    third = 2 * owner_rows // 5
    small = owner_rows - 2 * third
    slices = 2 * pl.cdiv(pairs, 2 * DEPTH)
    steps = 2 * slices + slices // 2
    chunks = pltpu.VMEM((steps, 2 * third, DEPTH), F32)
    near_rows = 8 * third + 8 * small
    far_rows = 4 * third
    dma = pltpu.SemaphoreType.DMA
    any_spec = pl.BlockSpec(memory_space=pl.ANY)
    return pl.pallas_call(
        functools.partial(cycle_kernel, wides),
        out_shape=jax.ShapeDtypeStruct((owner_rows, cols), F32),
        in_specs=[any_spec, any_spec],
        out_specs=pl.BlockSpec(memory_space=pltpu.VMEM),
        scratch_shapes=[
            pltpu.VMEM((rows, pairs), F32),
            chunks, chunks, chunks, chunks,
            pltpu.VMEM((slices, DEPTH, cols), F32),
            pltpu.VMEM((slices, DEPTH, cols), BF16),
            pltpu.VMEM((slices, DEPTH, cols), BF16),
            pltpu.VMEM((near_rows, cols), F32),
            pltpu.VMEM((near_rows, cols), F32),
            pltpu.VMEM((far_rows, cols), F32),
            pltpu.VMEM((far_rows, cols), F32),
            pltpu.VMEM((far_rows, cols), F32),
            pltpu.VMEM((4, 2, 2, third, cols), F32),
            pltpu.VMEM((4, 2, small, cols), F32),
            pltpu.VMEM((2, wides, third, cols), F32),
            pltpu.VMEM((wides, small, cols), F32),
            dma, dma((slices,)), dma((steps,)), dma((steps,)), dma((steps,)), dma((steps,)),
            dma, dma, dma((4, 2, 3)), dma((3, wides)),
        ],
        compiler_params=pltpu.CompilerParams(
            collective_id=0, has_side_effects=True, vmem_limit_bytes=60 * 1024 * 1024
        ),
        cost_estimate=pl.CostEstimate(
            flops=6 * 4 * rows * pairs * cols,
            bytes_accessed=4 * pairs * (rows + cols),
            transcendentals=0,
        ),
    )(amplitudes, integrals)


def plain_term(amplitudes, integrals):
    partial_term = jnp.dot(
        lax.all_gather(amplitudes, "narrow", axis=0, tiled=True),
        integrals,
        precision=lax.Precision.HIGHEST,
        preferred_element_type=F32,
    )
    return lax.psum_scatter(partial_term, "wide", scatter_dimension=0, tiled=True)


def per_device(wides, narrows, amplitudes, integrals, occupied_energy, virtual_energy_rows, virtual_energy_cols):
    rows = amplitudes.shape[0]
    if narrows == 4 and wides == 8 and rows % 20 == 0:
        cycle_term = fused_term(amplitudes, integrals, wides)
    else:
        cycle_term = plain_term(amplitudes, integrals)
    row_count = cycle_term.shape[0]
    col_count = cycle_term.shape[1]
    row_first = lax.axis_index("wide") * row_count
    col_first = lax.axis_index("narrow") * col_count
    row_energy = (occupied_energy[None, :] - virtual_energy_rows[:, None]).reshape(-1)
    col_energy = (occupied_energy[None, :] - virtual_energy_cols[:, None]).reshape(-1)
    row_part = lax.dynamic_slice_in_dim(row_energy, row_first, row_count)
    col_part = lax.dynamic_slice_in_dim(col_energy, col_first, col_count)
    denominator = row_part[:, None] + col_part[None, :]
    return cycle_term / denominator


def solution(mesh):
    in_specs = (P("narrow", "wide"), P("wide", "narrow"), P(), P(), P())
    out_specs = P("wide", "narrow")
    body = functools.partial(per_device, mesh.shape["wide"], mesh.shape["narrow"])
    return jax.shard_map(
        body, mesh=mesh, in_specs=in_specs, out_specs=out_specs, check_vma=False
    )
```

```python
import functools

import jax
import jax.numpy as jnp
from jax import lax
from jax.experimental import pallas as pl
from jax.experimental.pallas import tpu as pltpu
from jax.sharding import PartitionSpec as P

MESH = pl.DeviceIdType.MESH
F32 = jnp.float32
BF16 = jnp.bfloat16
DEPTH = 1152
BLOCK = 80


def halves(values):
    high = values.astype(BF16)
    return high, (values - high.astype(F32)).astype(BF16)


def by_rows(left, right):
    return lax.dot_general(
        left, right, (((1,), (1,)), ((), ())), preferred_element_type=F32
    )


def cycle_kernel(
    wides, amp, ints, out,
    own, mine, twin, far, far_twin, wide_ints, ints_high, ints_low,
    even, odd, group_sum, last_even, last_odd,
    send_big, send_small, recv_big, recv_small,
    own_sem, ints_sem, far_send, far_recv, pass_send, pass_recv, twin_send, twin_recv,
    sum_send, sum_recv,
):
    rows, pairs = amp.shape
    owner_rows = rows // 2
    third = 2 * owner_rows // 5
    small = owner_rows - 2 * third
    steps = mine.shape[0]
    slices = ints_high.shape[0]
    me = lax.axis_index("wide")
    narrow = lax.axis_index("narrow")
    across = lax.div(narrow, 2)
    core = lax.rem(narrow, 2)
    sibling = narrow + 1 - 2 * core
    neighbour = narrow + 2 - 4 * across
    diagonal = sibling + 2 - 4 * across
    shards = (narrow, sibling, neighbour, diagonal)

    own_copy = pltpu.make_async_copy(amp, own, own_sem)
    own_copy.start()

    def ints_copy(b):
        part = pl.ds(b * BLOCK, BLOCK)
        return pltpu.make_async_copy(ints.at[part], wide_ints.at[part], ints_sem.at[b])

    blocks = ints.shape[0] // BLOCK
    for b in range(blocks):
        ints_copy(b).start()

    barrier = pltpu.get_barrier_semaphore()
    for other in (sibling, neighbour):
        pl.semaphore_signal(barrier, inc=1, device_id=(me, other), device_id_type=MESH)
    for hop in range(1, wides):
        pl.semaphore_signal(
            barrier, inc=1, device_id=(lax.rem(me + hop, wides), narrow), device_id_type=MESH
        )
    pl.semaphore_wait(barrier, wides + 1)

    def far_copy(i):
        return pltpu.make_async_remote_copy(
            src_ref=mine.at[i], dst_ref=far.at[i],
            send_sem=far_send.at[i], recv_sem=far_recv.at[i],
            device_id=(me, neighbour), device_id_type=MESH,
        )

    def pass_copy(i):
        return pltpu.make_async_remote_copy(
            src_ref=far.at[i], dst_ref=far_twin.at[i],
            send_sem=pass_send.at[i], recv_sem=pass_recv.at[i],
            device_id=(me, sibling), device_id_type=MESH,
        )

    twin_copy = pltpu.make_async_remote_copy(
        src_ref=mine, dst_ref=twin, send_sem=twin_send, recv_sem=twin_recv,
        device_id=(me, sibling), device_id_type=MESH,
    )

    def pack(i, at, first, count, k):
        length = min(DEPTH, pairs - k * DEPTH)
        mine[i, at:at + count, :length] = own[first:first + count, k * DEPTH:k * DEPTH + length]
        if length < DEPTH:
            mine[i, at:at + count, length:] = jnp.zeros((count, DEPTH - length), F32)

    own_copy.wait()
    for g in range(2):
        for k in range(slices):
            i = g * slices + k
            pack(i, 0, g * third, third, k)
            pack(i, third, owner_rows + g * third, third, k)
            far_copy(i).start()
    for j in range(slices // 2):
        i = 2 * slices + j
        for p in range(2):
            pack(i, 2 * small * p, 2 * third, small, 2 * j + p)
            pack(i, 2 * small * p + small, owner_rows + 2 * third, small, 2 * j + p)
        far_copy(i).start()
    twin_copy.start()

    def sum_copy(s, h, g):
        owner = 2 * shards[s] + h
        src = send_big.at[s, h, g] if g < 2 else send_small.at[s, h]
        dst = recv_big.at[g, me] if g < 2 else recv_small.at[me]
        copy = pltpu.make_async_remote_copy(
            src_ref=src, dst_ref=dst,
            send_sem=sum_send.at[s, h, g], recv_sem=sum_recv.at[g, me],
            device_id=(owner, narrow), device_id_type=MESH,
        )
        return owner, copy

    def emit(s, h, g, value):
        if g < 2:
            send_big[s, h, g] = value
        else:
            send_small[s, h] = value
        owner, copy = sum_copy(s, h, g)

        @pl.when(owner == me)
        def _():
            if g < 2:
                recv_big[g, me] = value
            else:
                recv_small[me] = value

        @pl.when(owner != me)
        def _():
            copy.start()

    def product(values, k):
        high, low = halves(values)
        count = values.shape[0]
        both = by_rows(jnp.concatenate([high, low], axis=0), ints_high[k])
        rest = by_rows(high, ints_low[k])
        return both[:count] + (both[count:] + rest)

    even[...] = jnp.zeros_like(even)
    odd[...] = jnp.zeros_like(odd)

    def split_block(b, carry):
        ints_copy(b).wait()

        def split(t, inner):
            part = pl.ds(pl.multiple_of(b * BLOCK + t * 16, 16), 16)
            for k in range(slices):
                length = min(DEPTH, pairs - k * DEPTH)
                high, low = halves(wide_ints[part, k * DEPTH:k * DEPTH + length])
                ints_high[k, part, :length] = high
                ints_low[k, part, :length] = low
                if length < DEPTH:
                    nothing = jnp.zeros((16, DEPTH - length), BF16)
                    ints_high[k, part, length:] = nothing
                    ints_low[k, part, length:] = nothing
            return inner

        return lax.fori_loop(0, BLOCK // 16, split, carry)

    lax.fori_loop(0, blocks, split_block, 0)
    twin_copy.wait_recv()

    def near_step(j, carry):
        for p, total in ((0, even), (1, odd)):
            k = 2 * j + p
            parts = [
                mine[k], mine[slices + k], twin[k], twin[slices + k],
                mine[2 * slices + j], twin[2 * slices + j],
            ]
            total[...] += product(jnp.concatenate(parts, axis=0), k)
        return carry

    lax.fori_loop(0, slices // 2, near_step, 0)
    for s in range(2):
        for h in range(2):
            for g in range(2):
                at = 4 * third * s + 2 * third * g + third * h
                emit(s, h, g, even[at:at + third] + odd[at:at + third])
            at = 8 * third + 4 * small * s + small * h
            emit(s, h, 2, even[at:at + small] + odd[at + 2 * small:at + 3 * small])

    def arrive(i):
        far_copy(i).wait_recv()
        pass_copy(i).start()

    def far_block(i):
        pass_copy(i).wait_recv()
        return jnp.concatenate([far[i], far_twin[i]], axis=0)

    arrive(0)
    for g in range(2):
        group_sum[...] = jnp.zeros_like(group_sum)

        def far_step(k, carry):
            arrive(g * slices + k + 1)
            group_sum[...] += product(far_block(g * slices + k), k)
            return carry

        lax.fori_loop(0, slices, far_step, 0)
        for s in range(2):
            for h in range(2):
                at = 2 * third * s + third * h
                emit(2 + s, h, g, group_sum[at:at + third])

    last_even[...] = jnp.zeros_like(last_even)
    last_odd[...] = jnp.zeros_like(last_odd)

    def last_step(j, carry):
        @pl.when(j < slices // 2 - 1)
        def _():
            arrive(2 * slices + j + 1)

        block = far_block(2 * slices + j)
        last_even[...] += product(block, 2 * j)
        last_odd[...] += product(block, 2 * j + 1)
        return carry

    lax.fori_loop(0, slices // 2, last_step, 0)
    for s in range(2):
        for h in range(2):
            at = 4 * small * s + small * h
            emit(2 + s, h, 2, last_even[at:at + small] + last_odd[at + 2 * small:at + 3 * small])

    def drain(i, carry):
        far_copy(i).wait_send()
        pass_copy(i).wait_send()
        return carry

    lax.fori_loop(0, steps, drain, 0)
    twin_copy.wait_send()

    for g in range(3):
        for source in range(wides):
            @pl.when(me != source)
            def _():
                dst = recv_big.at[g, source] if g < 2 else recv_small.at[source]
                pltpu.make_async_remote_copy(
                    src_ref=dst, dst_ref=dst,
                    send_sem=sum_send.at[0, 0, g], recv_sem=sum_recv.at[g, source],
                    device_id=(source, narrow), device_id_type=MESH,
                ).wait_recv()
        held = recv_big.at[g] if g < 2 else recv_small
        total = held[0]
        for source in range(1, wides):
            total = total + held[source]
        out[g * third:g * third + total.shape[0], :] = total

    for s in range(4):
        for h in range(2):
            for g in range(3):
                owner, copy = sum_copy(s, h, g)

                @pl.when(owner != me)
                def _():
                    copy.wait_send()


def fused_term(amplitudes, integrals, wides):
    rows, pairs = amplitudes.shape
    cols = integrals.shape[1]
    owner_rows = rows // 2
    third = 2 * owner_rows // 5
    small = owner_rows - 2 * third
    slices = 2 * pl.cdiv(pairs, 2 * DEPTH)
    steps = 2 * slices + slices // 2
    chunks = pltpu.VMEM((steps, 2 * third, DEPTH), F32)
    near_rows = 8 * third + 8 * small
    far_rows = 4 * third
    dma = pltpu.SemaphoreType.DMA
    any_spec = pl.BlockSpec(memory_space=pl.ANY)
    return pl.pallas_call(
        functools.partial(cycle_kernel, wides),
        out_shape=jax.ShapeDtypeStruct((owner_rows, cols), F32),
        in_specs=[any_spec, any_spec],
        out_specs=pl.BlockSpec(memory_space=pltpu.VMEM),
        scratch_shapes=[
            pltpu.VMEM((rows, pairs), F32),
            chunks, chunks, chunks, chunks,
            pltpu.VMEM((cols, pairs), F32),
            pltpu.VMEM((slices, cols, DEPTH), BF16),
            pltpu.VMEM((slices, cols, DEPTH), BF16),
            pltpu.VMEM((near_rows, cols), F32),
            pltpu.VMEM((near_rows, cols), F32),
            pltpu.VMEM((far_rows, cols), F32),
            pltpu.VMEM((far_rows, cols), F32),
            pltpu.VMEM((far_rows, cols), F32),
            pltpu.VMEM((4, 2, 2, third, cols), F32),
            pltpu.VMEM((4, 2, small, cols), F32),
            pltpu.VMEM((2, wides, third, cols), F32),
            pltpu.VMEM((wides, small, cols), F32),
            dma, dma((cols // BLOCK,)), dma((steps,)), dma((steps,)), dma((steps,)), dma((steps,)),
            dma, dma, dma((4, 2, 3)), dma((3, wides)),
        ],
        compiler_params=pltpu.CompilerParams(
            collective_id=0, has_side_effects=True, vmem_limit_bytes=60 * 1024 * 1024
        ),
        cost_estimate=pl.CostEstimate(
            flops=6 * 4 * rows * pairs * cols,
            bytes_accessed=4 * pairs * (rows + cols),
            transcendentals=0,
        ),
    )(amplitudes, integrals.T)


def plain_term(amplitudes, integrals):
    partial_term = jnp.dot(
        lax.all_gather(amplitudes, "narrow", axis=0, tiled=True),
        integrals,
        precision=lax.Precision.HIGHEST,
        preferred_element_type=F32,
    )
    return lax.psum_scatter(partial_term, "wide", scatter_dimension=0, tiled=True)


def per_device(wides, narrows, amplitudes, integrals, occupied_energy, virtual_energy_rows, virtual_energy_cols):
    rows = amplitudes.shape[0]
    if narrows == 4 and wides == 8 and rows % 20 == 0 and integrals.shape[1] % BLOCK == 0:
        cycle_term = fused_term(amplitudes, integrals, wides)
    else:
        cycle_term = plain_term(amplitudes, integrals)
    row_count = cycle_term.shape[0]
    col_count = cycle_term.shape[1]
    row_first = lax.axis_index("wide") * row_count
    col_first = lax.axis_index("narrow") * col_count
    row_energy = (occupied_energy[None, :] - virtual_energy_rows[:, None]).reshape(-1)
    col_energy = (occupied_energy[None, :] - virtual_energy_cols[:, None]).reshape(-1)
    row_part = lax.dynamic_slice_in_dim(row_energy, row_first, row_count)
    col_part = lax.dynamic_slice_in_dim(col_energy, col_first, col_count)
    denominator = row_part[:, None] + col_part[None, :]
    return cycle_term / denominator


def solution(mesh):
    in_specs = (P("narrow", "wide"), P("wide", "narrow"), P(), P(), P())
    out_specs = P("wide", "narrow")
    body = functools.partial(per_device, mesh.shape["wide"], mesh.shape["narrow"])
    return jax.shard_map(
        body, mesh=mesh, in_specs=in_specs, out_specs=out_specs, check_vma=False
    )
```

```python
import functools

import jax
import jax.numpy as jnp
from jax import lax
from jax.experimental import pallas as pl
from jax.experimental.pallas import tpu as pltpu
from jax.sharding import PartitionSpec as P

MESH = pl.DeviceIdType.MESH
F32 = jnp.float32
BF16 = jnp.bfloat16
DEPTH = 1152
AHEAD = 4
BLOCK = 80


def halves(values):
    high = values.astype(BF16)
    return high, (values - high.astype(F32)).astype(BF16)


def by_rows(left, right):
    return lax.dot_general(
        left, right, (((1,), (1,)), ((), ())), preferred_element_type=F32
    )


def cycle_kernel(
    wides, amp, ints, occupied, virtual_rows, virtual_cols, out,
    own, mine, twin, far, far_twin, wide_ints, ints_high, ints_low,
    even, odd, group_sum, last_even, last_odd,
    send_big, send_small, recv_big, recv_small,
    own_sem, ints_sem, far_send, far_recv, pass_send, pass_recv, twin_send, twin_recv,
    sum_send, sum_recv,
    occupied_lanes, occupied_cells, rows_cells, cols_cells, col_part, bottom, energy_sem,
):
    rows, pairs = amp.shape
    owner_rows = rows // 2
    third = 2 * owner_rows // 5
    small = owner_rows - 2 * third
    steps = mine.shape[0]
    slices = ints_high.shape[0]
    me = lax.axis_index("wide")
    narrow = lax.axis_index("narrow")
    across = lax.div(narrow, 2)
    core = lax.rem(narrow, 2)
    sibling = narrow + 1 - 2 * core
    neighbour = narrow + 2 - 4 * across
    diagonal = sibling + 2 - 4 * across
    shards = (narrow, sibling, neighbour, diagonal)

    own_copy = pltpu.make_async_copy(amp, own, own_sem)
    own_copy.start()

    def ints_copy(b):
        part = pl.ds(b * BLOCK, BLOCK)
        return pltpu.make_async_copy(ints.at[part], wide_ints.at[part], ints_sem.at[b])

    energies = (
        (occupied, occupied_lanes), (occupied, occupied_cells),
        (virtual_rows, rows_cells), (virtual_cols, cols_cells),
    )
    energy_copies = [
        pltpu.make_async_copy(src, dst, energy_sem.at[e]) for e, (src, dst) in enumerate(energies)
    ]
    for copy in energy_copies:
        copy.start()
    blocks = ints.shape[0] // BLOCK
    for b in range(blocks):
        ints_copy(b).start()

    barrier = pltpu.get_barrier_semaphore()
    for other in (sibling, neighbour):
        pl.semaphore_signal(barrier, inc=1, device_id=(me, other), device_id_type=MESH)
    for hop in range(1, wides):
        pl.semaphore_signal(
            barrier, inc=1, device_id=(lax.rem(me + hop, wides), narrow), device_id_type=MESH
        )
    pl.semaphore_wait(barrier, wides + 1)

    def far_copy(i):
        return pltpu.make_async_remote_copy(
            src_ref=mine.at[i], dst_ref=far.at[i],
            send_sem=far_send.at[i], recv_sem=far_recv.at[i],
            device_id=(me, neighbour), device_id_type=MESH,
        )

    def pass_copy(i):
        return pltpu.make_async_remote_copy(
            src_ref=far.at[i], dst_ref=far_twin.at[i],
            send_sem=pass_send.at[i], recv_sem=pass_recv.at[i],
            device_id=(me, sibling), device_id_type=MESH,
        )

    twin_copy = pltpu.make_async_remote_copy(
        src_ref=mine, dst_ref=twin, send_sem=twin_send, recv_sem=twin_recv,
        device_id=(me, sibling), device_id_type=MESH,
    )

    def pack(i, at, first, count, k):
        length = min(DEPTH, pairs - k * DEPTH)
        mine[i, at:at + count, :length] = own[first:first + count, k * DEPTH:k * DEPTH + length]
        if length < DEPTH:
            mine[i, at:at + count, length:] = jnp.zeros((count, DEPTH - length), F32)

    own_copy.wait()
    for g in range(2):
        for k in range(slices):
            i = g * slices + k
            pack(i, 0, g * third, third, k)
            pack(i, third, owner_rows + g * third, third, k)
            if i < AHEAD // 2:
                far_copy(i).start()
    for j in range(slices // 2):
        i = 2 * slices + j
        for p in range(2):
            pack(i, 2 * small * p, 2 * third, small, 2 * j + p)
            pack(i, 2 * small * p + small, owner_rows + 2 * third, small, 2 * j + p)
    twin_copy.start()
    for i in range(AHEAD // 2, AHEAD):
        far_copy(i).start()

    occupied_count = occupied.shape[0]
    for copy in energy_copies:
        copy.wait()
    for b in range(ints.shape[0] // occupied_count):
        col_part[:, b * occupied_count:(b + 1) * occupied_count] = (
            occupied_lanes[...].reshape(1, occupied_count)
            - cols_cells[narrow * (ints.shape[0] // occupied_count) + b]
        )
    first = me * owner_rows
    virtual = rows_cells[lax.div(first, occupied_count)]
    for r in range(owner_rows):
        row_part = occupied_cells[lax.rem(first, occupied_count) + r] - virtual
        bottom[r:r + 1, :] = row_part + col_part[...]

    def sum_copy(s, h, g):
        owner = 2 * shards[s] + h
        src = send_big.at[s, h, g] if g < 2 else send_small.at[s, h]
        dst = recv_big.at[g, me] if g < 2 else recv_small.at[me]
        copy = pltpu.make_async_remote_copy(
            src_ref=src, dst_ref=dst,
            send_sem=sum_send.at[s, h, g], recv_sem=sum_recv.at[g, me],
            device_id=(owner, narrow), device_id_type=MESH,
        )
        return owner, copy

    def emit(s, h, g, value):
        if g < 2:
            send_big[s, h, g] = value
        else:
            send_small[s, h] = value
        owner, copy = sum_copy(s, h, g)

        @pl.when(owner == me)
        def _():
            if g < 2:
                recv_big[g, me] = value
            else:
                recv_small[me] = value

        @pl.when(owner != me)
        def _():
            copy.start()

    def product(values, k):
        high, low = halves(values)
        count = values.shape[0]
        both = by_rows(jnp.concatenate([high, low], axis=0), ints_high[k])
        rest = by_rows(high, ints_low[k])
        return both[:count] + (both[count:] + rest)

    even[...] = jnp.zeros_like(even)
    odd[...] = jnp.zeros_like(odd)

    def split_block(b, carry):
        ints_copy(b).wait()

        def split(t, inner):
            part = pl.ds(pl.multiple_of(b * BLOCK + t * 16, 16), 16)
            for k in range(slices):
                length = min(DEPTH, pairs - k * DEPTH)
                high, low = halves(wide_ints[part, k * DEPTH:k * DEPTH + length])
                ints_high[k, part, :length] = high
                ints_low[k, part, :length] = low
                if length < DEPTH:
                    nothing = jnp.zeros((16, DEPTH - length), BF16)
                    ints_high[k, part, length:] = nothing
                    ints_low[k, part, length:] = nothing
            return inner

        lax.fori_loop(0, BLOCK // 16, split, 0)

        @pl.when(lax.rem(b, 2) == 1)
        def _():
            far_copy(AHEAD + lax.div(b, 2)).start()

        return carry

    lax.fori_loop(0, blocks, split_block, 0)
    twin_copy.wait_recv()

    early = AHEAD + blocks // 2
    issued = early + slices // 2

    def near_step(j, carry):
        for p, total in ((0, even), (1, odd)):
            k = 2 * j + p
            parts = [
                mine[k], mine[slices + k], twin[k], twin[slices + k],
                mine[2 * slices + j], twin[2 * slices + j],
            ]
            total[...] += product(jnp.concatenate(parts, axis=0), k)
        far_copy(early + j).start()
        return carry

    lax.fori_loop(0, slices // 2, near_step, 0)
    for s in range(2):
        for h in range(2):
            for g in range(2):
                at = 4 * third * s + 2 * third * g + third * h
                emit(s, h, g, even[at:at + third] + odd[at:at + third])
            at = 8 * third + 4 * small * s + small * h
            emit(s, h, 2, even[at:at + small] + odd[at + 2 * small:at + 3 * small])

    def arrive(i):
        far_copy(i).wait_recv()
        pass_copy(i).start()

        @pl.when((i >= issued - AHEAD) & (i < steps - AHEAD))
        def _():
            far_copy(i + AHEAD).start()

    def far_block(i):
        pass_copy(i).wait_recv()
        return jnp.concatenate([far[i], far_twin[i]], axis=0)

    arrive(0)
    for g in range(2):
        group_sum[...] = jnp.zeros_like(group_sum)

        def far_step(k, carry):
            arrive(g * slices + k + 1)
            group_sum[...] += product(far_block(g * slices + k), k)
            return carry

        lax.fori_loop(0, slices, far_step, 0)
        for s in range(2):
            for h in range(2):
                at = 2 * third * s + third * h
                emit(2 + s, h, g, group_sum[at:at + third])

    last_even[...] = jnp.zeros_like(last_even)
    last_odd[...] = jnp.zeros_like(last_odd)

    def last_step(j, carry):
        @pl.when(j < slices // 2 - 1)
        def _():
            arrive(2 * slices + j + 1)

        block = far_block(2 * slices + j)
        last_even[...] += product(block, 2 * j)
        last_odd[...] += product(block, 2 * j + 1)
        return carry

    lax.fori_loop(0, slices // 2, last_step, 0)
    for s in range(2):
        for h in range(2):
            at = 4 * small * s + small * h
            emit(2 + s, h, 2, last_even[at:at + small] + last_odd[at + 2 * small:at + 3 * small])

    def drain(i, carry):
        far_copy(i).wait_send()
        pass_copy(i).wait_send()
        return carry

    lax.fori_loop(0, steps, drain, 0)
    twin_copy.wait_send()

    for g in range(3):
        for source in range(wides):
            @pl.when(me != source)
            def _():
                dst = recv_big.at[g, source] if g < 2 else recv_small.at[source]
                pltpu.make_async_remote_copy(
                    src_ref=dst, dst_ref=dst,
                    send_sem=sum_send.at[0, 0, g], recv_sem=sum_recv.at[g, source],
                    device_id=(source, narrow), device_id_type=MESH,
                ).wait_recv()
        held = recv_big.at[g] if g < 2 else recv_small
        total = held[0]
        for source in range(1, wides):
            total = total + held[source]
        part = pl.ds(g * third, total.shape[0])
        out[part, :] = total / bottom[part, :]

    for s in range(4):
        for h in range(2):
            for g in range(3):
                owner, copy = sum_copy(s, h, g)

                @pl.when(owner != me)
                def _():
                    copy.wait_send()


def fused_step(wides, amplitudes, integrals, occupied, virtual_rows, virtual_cols):
    rows, pairs = amplitudes.shape
    cols = integrals.shape[1]
    owner_rows = rows // 2
    third = 2 * owner_rows // 5
    small = owner_rows - 2 * third
    slices = 2 * pl.cdiv(pairs, 2 * DEPTH)
    steps = 2 * slices + slices // 2
    chunks = pltpu.VMEM((steps, 2 * third, DEPTH), F32)
    near_rows = 8 * third + 8 * small
    far_rows = 4 * third
    dma = pltpu.SemaphoreType.DMA
    any_spec = pl.BlockSpec(memory_space=pl.ANY)
    return pl.pallas_call(
        functools.partial(cycle_kernel, wides),
        out_shape=jax.ShapeDtypeStruct((owner_rows, cols), F32),
        in_specs=[any_spec] * 5,
        out_specs=pl.BlockSpec(memory_space=pltpu.VMEM),
        scratch_shapes=[
            pltpu.VMEM((rows, pairs), F32),
            chunks, chunks, chunks, chunks,
            pltpu.VMEM((cols, pairs), F32),
            pltpu.VMEM((slices, cols, DEPTH), BF16),
            pltpu.VMEM((slices, cols, DEPTH), BF16),
            pltpu.VMEM((near_rows, cols), F32),
            pltpu.VMEM((near_rows, cols), F32),
            pltpu.VMEM((far_rows, cols), F32),
            pltpu.VMEM((far_rows, cols), F32),
            pltpu.VMEM((far_rows, cols), F32),
            pltpu.VMEM((4, 2, 2, third, cols), F32),
            pltpu.VMEM((4, 2, small, cols), F32),
            pltpu.VMEM((2, wides, third, cols), F32),
            pltpu.VMEM((wides, small, cols), F32),
            dma, dma((cols // BLOCK,)), dma((steps,)), dma((steps,)), dma((steps,)), dma((steps,)),
            dma, dma, dma((4, 2, 3)), dma((3, wides)),
            pltpu.VMEM(occupied.shape, F32),
            pltpu.SMEM(occupied.shape, F32),
            pltpu.SMEM(virtual_rows.shape, F32),
            pltpu.SMEM(virtual_cols.shape, F32),
            pltpu.VMEM((1, cols), F32),
            pltpu.VMEM((owner_rows, cols), F32),
            dma((4,)),
        ],
        compiler_params=pltpu.CompilerParams(
            collective_id=0, has_side_effects=True, vmem_limit_bytes=60 * 1024 * 1024
        ),
        cost_estimate=pl.CostEstimate(
            flops=6 * 4 * rows * pairs * cols,
            bytes_accessed=4 * pairs * (rows + cols),
            transcendentals=0,
        ),
    )(amplitudes, integrals.T, occupied, virtual_rows, virtual_cols)


def plain_term(amplitudes, integrals):
    partial_term = jnp.dot(
        lax.all_gather(amplitudes, "narrow", axis=0, tiled=True),
        integrals,
        precision=lax.Precision.HIGHEST,
        preferred_element_type=F32,
    )
    return lax.psum_scatter(partial_term, "wide", scatter_dimension=0, tiled=True)


def per_device(wides, narrows, amplitudes, integrals, occupied_energy, virtual_energy_rows, virtual_energy_cols):
    rows = amplitudes.shape[0]
    if narrows == 4 and wides == 8 and rows % 20 == 0 and integrals.shape[1] % BLOCK == 0:
        return fused_step(
            wides, amplitudes, integrals,
            occupied_energy, virtual_energy_rows, virtual_energy_cols,
        )
    cycle_term = plain_term(amplitudes, integrals)
    row_count = cycle_term.shape[0]
    col_count = cycle_term.shape[1]
    row_first = lax.axis_index("wide") * row_count
    col_first = lax.axis_index("narrow") * col_count
    row_energy = (occupied_energy[None, :] - virtual_energy_rows[:, None]).reshape(-1)
    col_energy = (occupied_energy[None, :] - virtual_energy_cols[:, None]).reshape(-1)
    row_part = lax.dynamic_slice_in_dim(row_energy, row_first, row_count)
    col_part = lax.dynamic_slice_in_dim(col_energy, col_first, col_count)
    denominator = row_part[:, None] + col_part[None, :]
    return cycle_term / denominator


def solution(mesh):
    in_specs = (P("narrow", "wide"), P("wide", "narrow"), P(), P(), P())
    out_specs = P("wide", "narrow")
    body = functools.partial(per_device, mesh.shape["wide"], mesh.shape["narrow"])
    return jax.shard_map(
        body, mesh=mesh, in_specs=in_specs, out_specs=out_specs, check_vma=False
    )
```

```python
import functools

import jax
import jax.numpy as jnp
from jax import lax
from jax.experimental import pallas as pl
from jax.experimental.pallas import tpu as pltpu
from jax.sharding import PartitionSpec as P

MESH = pl.DeviceIdType.MESH
F32 = jnp.float32
BF16 = jnp.bfloat16
DEPTH = 1152
AHEAD = 4
BLOCK = 80


def halves(values):
    high = values.astype(BF16)
    return high, (values - high.astype(F32)).astype(BF16)


def by_rows(left, right):
    return lax.dot_general(
        left, right, (((1,), (1,)), ((), ())), preferred_element_type=F32
    )


def cycle_kernel(
    wides, amp, ints, occupied, virtual_rows, virtual_cols, out,
    own, mine, twin, far, far_twin, wide_ints, ints_high, ints_low,
    even, odd, group_sum, far_even, far_odd,
    send_big, send_small, recv_big, recv_small,
    own_sem, ints_sem, far_send, far_recv, pass_send, pass_recv, twin_send, twin_recv,
    sum_send, sum_recv,
    occupied_lanes, occupied_cells, rows_cells, cols_cells, col_part, bottom, energy_sem,
):
    rows, pairs = amp.shape
    owner_rows = rows // 2
    third = 2 * owner_rows // 5
    small = owner_rows - 2 * third
    steps = mine.shape[0]
    slices = ints_high.shape[0]
    last_length = pl.cdiv(pairs - (slices - 1) * DEPTH, 128) * 128
    first_length = pl.cdiv(last_length, 256) * 128
    light = 3 * slices // 2
    me = lax.axis_index("wide")
    narrow = lax.axis_index("narrow")
    across = lax.div(narrow, 2)
    core = lax.rem(narrow, 2)
    sibling = narrow + 1 - 2 * core
    neighbour = narrow + 2 - 4 * across
    diagonal = sibling + 2 - 4 * across
    shards = (narrow, sibling, neighbour, diagonal)

    own_copy = pltpu.make_async_copy(amp, own, own_sem)
    own_copy.start()

    def ints_copy(b):
        part = pl.ds(b * BLOCK, BLOCK)
        return pltpu.make_async_copy(ints.at[part], wide_ints.at[part], ints_sem.at[b])

    energies = (
        (occupied, occupied_lanes), (occupied, occupied_cells),
        (virtual_rows, rows_cells), (virtual_cols, cols_cells),
    )
    energy_copies = [
        pltpu.make_async_copy(src, dst, energy_sem.at[e]) for e, (src, dst) in enumerate(energies)
    ]
    for copy in energy_copies:
        copy.start()
    blocks = ints.shape[0] // BLOCK

    barrier = pltpu.get_barrier_semaphore()
    for other in (sibling, neighbour):
        pl.semaphore_signal(barrier, inc=1, device_id=(me, other), device_id_type=MESH)
    for hop in range(1, wides):
        pl.semaphore_signal(
            barrier, inc=1, device_id=(lax.rem(me + hop, wides), narrow), device_id_type=MESH
        )
    pl.semaphore_wait(barrier, wides + 1)

    last_part = [(0, first_length), (first_length, last_length - first_length)]

    def chunk(buffer, i, piece):
        if piece is None:
            return buffer.at[i]
        return buffer.at[i, :, pl.ds(*last_part[piece])]

    def far_copy(i, piece=None):
        at = i + (piece or 0)
        return pltpu.make_async_remote_copy(
            src_ref=chunk(mine, i, piece), dst_ref=chunk(far, i, piece),
            send_sem=far_send.at[at], recv_sem=far_recv.at[at],
            device_id=(me, neighbour), device_id_type=MESH,
        )

    def pass_copy(i, piece=None):
        at = i + (piece or 0)
        return pltpu.make_async_remote_copy(
            src_ref=chunk(far, i, piece), dst_ref=chunk(far_twin, i, piece),
            send_sem=pass_send.at[at], recv_sem=pass_recv.at[at],
            device_id=(me, sibling), device_id_type=MESH,
        )

    twin_copy = pltpu.make_async_remote_copy(
        src_ref=mine, dst_ref=twin, send_sem=twin_send, recv_sem=twin_recv,
        device_id=(me, sibling), device_id_type=MESH,
    )

    def pack(i, at, first, count, k):
        length = min(DEPTH, pairs - k * DEPTH)
        mine[i, at:at + count, :length] = own[first:first + count, k * DEPTH:k * DEPTH + length]
        if length < DEPTH:
            mine[i, at:at + count, length:] = jnp.zeros((count, DEPTH - length), F32)

    own_copy.wait()
    for j in range(slices // 2):
        for p in range(2):
            pack(3 * j, 2 * small * p, 2 * third, small, 2 * j + p)
            pack(3 * j, 2 * small * p + small, owner_rows + 2 * third, small, 2 * j + p)
        for p in range(2):
            i = 3 * j + 1 + p
            pack(i, 0, 0, third, 2 * j + p)
            pack(i, third, owner_rows, third, 2 * j + p)
        if j == 0:
            for i in range(AHEAD // 2):
                far_copy(i).start()
            for b in range(blocks):
                ints_copy(b).start()
    for k in range(slices):
        pack(light + k, 0, third, third, k)
        pack(light + k, third, owner_rows + third, third, k)
    twin_copy.start()
    for i in range(AHEAD // 2, AHEAD):
        far_copy(i).start()

    occupied_count = occupied.shape[0]
    for copy in energy_copies:
        copy.wait()
    for b in range(ints.shape[0] // occupied_count):
        col_part[:, b * occupied_count:(b + 1) * occupied_count] = (
            occupied_lanes[...].reshape(1, occupied_count)
            - cols_cells[narrow * (ints.shape[0] // occupied_count) + b]
        )
    first = me * owner_rows
    virtual = rows_cells[lax.div(first, occupied_count)]
    for r in range(owner_rows):
        row_part = occupied_cells[lax.rem(first, occupied_count) + r] - virtual
        bottom[r:r + 1, :] = row_part + col_part[...]

    def sum_copy(s, h, g):
        owner = 2 * shards[s] + h
        src = send_big.at[s, h, g] if g < 2 else send_small.at[s, h]
        dst = recv_big.at[g, me] if g < 2 else recv_small.at[me]
        copy = pltpu.make_async_remote_copy(
            src_ref=src, dst_ref=dst,
            send_sem=sum_send.at[s, h, g], recv_sem=sum_recv.at[g, me],
            device_id=(owner, narrow), device_id_type=MESH,
        )
        return owner, copy

    def emit(s, h, g, value):
        if g < 2:
            send_big[s, h, g] = value
        else:
            send_small[s, h] = value
        owner, copy = sum_copy(s, h, g)

        @pl.when(owner == me)
        def _():
            if g < 2:
                recv_big[g, me] = value
            else:
                recv_small[me] = value

        @pl.when(owner != me)
        def _():
            copy.start()

    def product(values, k, part=(0, DEPTH)):
        high, low = halves(values)
        count = values.shape[0]
        both = by_rows(jnp.concatenate([high, low], axis=0), ints_high[k, :, pl.ds(*part)])
        rest = by_rows(high, ints_low[k, :, pl.ds(*part)])
        return both[:count] + (both[count:] + rest)

    even[...] = jnp.zeros_like(even)
    odd[...] = jnp.zeros_like(odd)

    def split_block(b, carry):
        ints_copy(b).wait()

        def split(t, inner):
            part = pl.ds(pl.multiple_of(b * BLOCK + t * 16, 16), 16)
            for k in range(slices):
                length = min(DEPTH, pairs - k * DEPTH)
                high, low = halves(wide_ints[part, k * DEPTH:k * DEPTH + length])
                ints_high[k, part, :length] = high
                ints_low[k, part, :length] = low
                if length < DEPTH:
                    nothing = jnp.zeros((16, DEPTH - length), BF16)
                    ints_high[k, part, length:] = nothing
                    ints_low[k, part, length:] = nothing
            return inner

        lax.fori_loop(0, BLOCK // 16, split, 0)

        @pl.when(lax.rem(b, 2) == 1)
        def _():
            far_copy(AHEAD + lax.div(b, 2)).start()

        return carry

    lax.fori_loop(0, blocks, split_block, 0)
    twin_copy.wait_recv()

    early = AHEAD + blocks // 2
    issued = early + slices // 2

    def near_step(j, carry):
        for p, total in ((0, even), (1, odd)):
            k = 2 * j + p
            parts = [
                mine[3 * j + 1 + p], mine[light + k], twin[3 * j + 1 + p], twin[light + k],
                mine[3 * j], twin[3 * j],
            ]
            total[...] += product(jnp.concatenate(parts, axis=0), k)
        far_copy(early + j).start()
        return carry

    lax.fori_loop(0, slices // 2, near_step, 0)
    for s in range(2):
        for h in range(2):
            for g in range(2):
                at = 4 * third * s + 2 * third * g + third * h
                emit(s, h, g, even[at:at + third] + odd[at:at + third])
            at = 8 * third + 4 * small * s + small * h
            emit(s, h, 2, even[at:at + small] + odd[at + 2 * small:at + 3 * small])

    def arrive(i):
        far_copy(i).wait_recv()
        pass_copy(i).start()

        @pl.when((i >= issued - AHEAD) & (i < steps - 1 - AHEAD))
        def _():
            far_copy(i + AHEAD).start()

        @pl.when(i == steps - 1 - AHEAD)
        def _():
            for piece in range(2):
                far_copy(steps - 1, piece).start()

    def arrive_last(piece):
        far_copy(steps - 1, piece).wait_recv()
        pass_copy(steps - 1, piece).start()

    far_even[...] = jnp.zeros_like(far_even)
    far_odd[...] = jnp.zeros_like(far_odd)
    arrive(0)
    arrive(1)

    def far_step(j, carry):
        arrive(3 * j + 2)
        pass_copy(3 * j).wait_recv()
        pass_copy(3 * j + 1).wait_recv()
        parts = [far[3 * j + 1], far_twin[3 * j + 1], far[3 * j], far_twin[3 * j]]
        far_even[...] += product(jnp.concatenate(parts, axis=0), 2 * j)
        arrive(3 * j + 3)

        @pl.when(j < slices // 2 - 1)
        def _():
            arrive(3 * j + 4)

        pass_copy(3 * j + 2).wait_recv()
        parts = [far[3 * j + 2], far_twin[3 * j + 2], far[3 * j], far_twin[3 * j]]
        far_odd[...] += product(jnp.concatenate(parts, axis=0), 2 * j + 1)
        return carry

    lax.fori_loop(0, slices // 2, far_step, 0)
    for s in range(2):
        for h in range(2):
            at = 2 * third * s + third * h
            emit(2 + s, h, 0, far_even[at:at + third] + far_odd[at:at + third])
            at = 4 * third + 4 * small * s + small * h
            emit(2 + s, h, 2, far_even[at:at + small] + far_odd[at + 2 * small:at + 3 * small])

    def light_product(k):
        pass_copy(light + k).wait_recv()
        group_sum[...] += product(
            jnp.concatenate([far[light + k], far_twin[light + k]], axis=0), k
        )

    def light_step(k, carry):
        arrive(light + k + 1)
        light_product(k)
        return carry

    group_sum[...] = jnp.zeros_like(group_sum)
    lax.fori_loop(0, slices - 2, light_step, 0)
    arrive_last(0)
    light_product(slices - 2)
    arrive_last(1)
    for piece in range(2):
        pass_copy(steps - 1, piece).wait_recv()
        part = pl.ds(*last_part[piece])
        group_sum[...] += product(
            jnp.concatenate([far[steps - 1, :, part], far_twin[steps - 1, :, part]], axis=0),
            slices - 1, last_part[piece],
        )
    for s in range(2):
        for h in range(2):
            at = 2 * third * s + third * h
            emit(2 + s, h, 1, group_sum[at:at + third])

    def drain(i, carry):
        far_copy(i).wait_send()
        pass_copy(i).wait_send()
        return carry

    lax.fori_loop(0, steps - 1, drain, 0)
    for piece in range(2):
        far_copy(steps - 1, piece).wait_send()
        pass_copy(steps - 1, piece).wait_send()
    twin_copy.wait_send()

    for g in range(3):
        for source in range(wides):
            @pl.when(me != source)
            def _():
                dst = recv_big.at[g, source] if g < 2 else recv_small.at[source]
                pltpu.make_async_remote_copy(
                    src_ref=dst, dst_ref=dst,
                    send_sem=sum_send.at[0, 0, g], recv_sem=sum_recv.at[g, source],
                    device_id=(source, narrow), device_id_type=MESH,
                ).wait_recv()
        held = recv_big.at[g] if g < 2 else recv_small
        total = held[0]
        for source in range(1, wides):
            total = total + held[source]
        part = pl.ds(g * third, total.shape[0])
        out[part, :] = total / bottom[part, :]

    for s in range(4):
        for h in range(2):
            for g in range(3):
                owner, copy = sum_copy(s, h, g)

                @pl.when(owner != me)
                def _():
                    copy.wait_send()


def fused_step(wides, amplitudes, integrals, occupied, virtual_rows, virtual_cols):
    rows, pairs = amplitudes.shape
    cols = integrals.shape[1]
    owner_rows = rows // 2
    third = 2 * owner_rows // 5
    small = owner_rows - 2 * third
    slices = 2 * pl.cdiv(pairs, 2 * DEPTH)
    steps = 2 * slices + slices // 2
    chunks = pltpu.VMEM((steps, 2 * third, DEPTH), F32)
    near_rows = 8 * third + 8 * small
    far_rows = 4 * third
    dma = pltpu.SemaphoreType.DMA
    any_spec = pl.BlockSpec(memory_space=pl.ANY)
    return pl.pallas_call(
        functools.partial(cycle_kernel, wides),
        out_shape=jax.ShapeDtypeStruct((owner_rows, cols), F32),
        in_specs=[any_spec] * 5,
        out_specs=pl.BlockSpec(memory_space=pltpu.VMEM),
        scratch_shapes=[
            pltpu.VMEM((rows, pairs), F32),
            chunks, chunks, chunks, chunks,
            pltpu.VMEM((cols, pairs), F32),
            pltpu.VMEM((slices, cols, DEPTH), BF16),
            pltpu.VMEM((slices, cols, DEPTH), BF16),
            pltpu.VMEM((near_rows, cols), F32),
            pltpu.VMEM((near_rows, cols), F32),
            pltpu.VMEM((far_rows, cols), F32),
            pltpu.VMEM((far_rows + 8 * small, cols), F32),
            pltpu.VMEM((far_rows + 8 * small, cols), F32),
            pltpu.VMEM((4, 2, 2, third, cols), F32),
            pltpu.VMEM((4, 2, small, cols), F32),
            pltpu.VMEM((2, wides, third, cols), F32),
            pltpu.VMEM((wides, small, cols), F32),
            dma, dma((cols // BLOCK,)), dma((steps + 1,)), dma((steps + 1,)),
            dma((steps + 1,)), dma((steps + 1,)),
            dma, dma, dma((4, 2, 3)), dma((3, wides)),
            pltpu.VMEM(occupied.shape, F32),
            pltpu.SMEM(occupied.shape, F32),
            pltpu.SMEM(virtual_rows.shape, F32),
            pltpu.SMEM(virtual_cols.shape, F32),
            pltpu.VMEM((1, cols), F32),
            pltpu.VMEM((owner_rows, cols), F32),
            dma((4,)),
        ],
        compiler_params=pltpu.CompilerParams(
            collective_id=0, has_side_effects=True, vmem_limit_bytes=60 * 1024 * 1024
        ),
        cost_estimate=pl.CostEstimate(
            flops=6 * 4 * rows * pairs * cols,
            bytes_accessed=4 * pairs * (rows + cols),
            transcendentals=0,
        ),
    )(amplitudes, integrals.T, occupied, virtual_rows, virtual_cols)


def plain_term(amplitudes, integrals):
    partial_term = jnp.dot(
        lax.all_gather(amplitudes, "narrow", axis=0, tiled=True),
        integrals,
        precision=lax.Precision.HIGHEST,
        preferred_element_type=F32,
    )
    return lax.psum_scatter(partial_term, "wide", scatter_dimension=0, tiled=True)


def per_device(wides, narrows, amplitudes, integrals, occupied_energy, virtual_energy_rows, virtual_energy_cols):
    rows = amplitudes.shape[0]
    if narrows == 4 and wides == 8 and rows % 20 == 0 and integrals.shape[1] % BLOCK == 0:
        return fused_step(
            wides, amplitudes, integrals,
            occupied_energy, virtual_energy_rows, virtual_energy_cols,
        )
    cycle_term = plain_term(amplitudes, integrals)
    row_count = cycle_term.shape[0]
    col_count = cycle_term.shape[1]
    row_first = lax.axis_index("wide") * row_count
    col_first = lax.axis_index("narrow") * col_count
    row_energy = (occupied_energy[None, :] - virtual_energy_rows[:, None]).reshape(-1)
    col_energy = (occupied_energy[None, :] - virtual_energy_cols[:, None]).reshape(-1)
    row_part = lax.dynamic_slice_in_dim(row_energy, row_first, row_count)
    col_part = lax.dynamic_slice_in_dim(col_energy, col_first, col_count)
    denominator = row_part[:, None] + col_part[None, :]
    return cycle_term / denominator


def solution(mesh):
    in_specs = (P("narrow", "wide"), P("wide", "narrow"), P(), P(), P())
    out_specs = P("wide", "narrow")
    body = functools.partial(per_device, mesh.shape["wide"], mesh.shape["narrow"])
    return jax.shard_map(
        body, mesh=mesh, in_specs=in_specs, out_specs=out_specs, check_vma=False
    )
```

```python
import functools

import jax
import jax.numpy as jnp
from jax import lax
from jax.experimental import pallas as pl
from jax.experimental.pallas import tpu as pltpu
from jax.sharding import PartitionSpec as P

MESH = pl.DeviceIdType.MESH
F32 = jnp.float32
BF16 = jnp.bfloat16
DEPTH = 1152
AHEAD = 4
BLOCK = 80


def halves(values):
    high = values.astype(BF16)
    return high, (values - high.astype(F32)).astype(BF16)


def by_rows(left, right):
    return lax.dot_general(
        left, right, (((1,), (1,)), ((), ())), preferred_element_type=F32
    )


def cycle_kernel(
    wides, amp, ints, occupied, virtual_rows, virtual_cols, out,
    own, mine, twin, far, far_twin, wide_ints, ints_high, ints_low,
    even, odd, group_sum, far_even, far_odd,
    send_big, send_small, recv_big, recv_small,
    own_sem, ints_sem, far_send, far_recv, pass_send, pass_recv, twin_send, twin_recv,
    sum_send, sum_recv,
    occupied_lanes, occupied_cells, rows_cells, cols_cells, col_part, bottom, energy_sem, result, out_sem,
):
    rows, pairs = amp.shape
    owner_rows = rows // 2
    third = 2 * owner_rows // 5
    small = owner_rows - 2 * third
    steps = mine.shape[0]
    slices = ints_high.shape[0]
    last_length = pl.cdiv(pairs - (slices - 1) * DEPTH, 128) * 128
    first_length = pl.cdiv(last_length, 256) * 128
    light = 3 * slices // 2
    me = lax.axis_index("wide")
    narrow = lax.axis_index("narrow")
    across = lax.div(narrow, 2)
    core = lax.rem(narrow, 2)
    sibling = narrow + 1 - 2 * core
    neighbour = narrow + 2 - 4 * across
    diagonal = sibling + 2 - 4 * across
    shards = (narrow, sibling, neighbour, diagonal)

    own_copy = pltpu.make_async_copy(amp, own, own_sem)
    own_copy.start()

    def ints_copy(b):
        part = pl.ds(b * BLOCK, BLOCK)
        return pltpu.make_async_copy(ints.at[part], wide_ints.at[part], ints_sem.at[b])

    energies = (
        (occupied, occupied_lanes), (occupied, occupied_cells),
        (virtual_rows, rows_cells), (virtual_cols, cols_cells),
    )
    energy_copies = [
        pltpu.make_async_copy(src, dst, energy_sem.at[e]) for e, (src, dst) in enumerate(energies)
    ]
    for copy in energy_copies:
        copy.start()
    blocks = ints.shape[0] // BLOCK

    barrier = pltpu.get_barrier_semaphore()
    for other in (sibling, neighbour):
        pl.semaphore_signal(barrier, inc=1, device_id=(me, other), device_id_type=MESH)
    for hop in range(1, wides):
        pl.semaphore_signal(
            barrier, inc=1, device_id=(lax.rem(me + hop, wides), narrow), device_id_type=MESH
        )
    pl.semaphore_wait(barrier, wides + 1)

    last_part = [(0, first_length), (first_length, last_length - first_length)]

    def chunk(buffer, i, piece):
        if piece is None:
            return buffer.at[i]
        return buffer.at[i, :, pl.ds(*last_part[piece])]

    def far_copy(i, piece=None):
        at = i + (piece or 0)
        return pltpu.make_async_remote_copy(
            src_ref=chunk(mine, i, piece), dst_ref=chunk(far, i, piece),
            send_sem=far_send.at[at], recv_sem=far_recv.at[at],
            device_id=(me, neighbour), device_id_type=MESH,
        )

    def pass_copy(i, piece=None):
        at = i + (piece or 0)
        return pltpu.make_async_remote_copy(
            src_ref=chunk(far, i, piece), dst_ref=chunk(far_twin, i, piece),
            send_sem=pass_send.at[at], recv_sem=pass_recv.at[at],
            device_id=(me, sibling), device_id_type=MESH,
        )

    twin_copy = pltpu.make_async_remote_copy(
        src_ref=mine, dst_ref=twin, send_sem=twin_send, recv_sem=twin_recv,
        device_id=(me, sibling), device_id_type=MESH,
    )

    def pack(i, at, first, count, k):
        length = min(DEPTH, pairs - k * DEPTH)
        mine[i, at:at + count, :length] = own[first:first + count, k * DEPTH:k * DEPTH + length]
        if length < DEPTH:
            mine[i, at:at + count, length:] = jnp.zeros((count, DEPTH - length), F32)

    own_copy.wait()
    for j in range(slices // 2):
        for p in range(2):
            pack(3 * j, 2 * small * p, 2 * third, small, 2 * j + p)
            pack(3 * j, 2 * small * p + small, owner_rows + 2 * third, small, 2 * j + p)
        for p in range(2):
            i = 3 * j + 1 + p
            pack(i, 0, 0, third, 2 * j + p)
            pack(i, third, owner_rows, third, 2 * j + p)
        if j == 0:
            for i in range(AHEAD // 2):
                far_copy(i).start()
            for b in range(blocks):
                ints_copy(b).start()
    for k in range(slices):
        pack(light + k, 0, third, third, k)
        pack(light + k, third, owner_rows + third, third, k)
    twin_copy.start()
    for i in range(AHEAD // 2, AHEAD):
        far_copy(i).start()

    occupied_count = occupied.shape[0]
    for copy in energy_copies:
        copy.wait()
    for b in range(ints.shape[0] // occupied_count):
        col_part[:, b * occupied_count:(b + 1) * occupied_count] = (
            occupied_lanes[...].reshape(1, occupied_count)
            - cols_cells[narrow * (ints.shape[0] // occupied_count) + b]
        )
    first = me * owner_rows
    virtual = rows_cells[lax.div(first, occupied_count)]
    for r in range(owner_rows):
        row_part = occupied_cells[lax.rem(first, occupied_count) + r] - virtual
        bottom[r:r + 1, :] = row_part + col_part[...]

    def sum_copy(s, h, g):
        owner = 2 * shards[s] + h
        src = send_big.at[s, h, g] if g < 2 else send_small.at[s, h]
        dst = recv_big.at[g, me] if g < 2 else recv_small.at[me]
        copy = pltpu.make_async_remote_copy(
            src_ref=src, dst_ref=dst,
            send_sem=sum_send.at[s, h, g], recv_sem=sum_recv.at[g, me],
            device_id=(owner, narrow), device_id_type=MESH,
        )
        return owner, copy

    def emit(s, h, g, value):
        if g < 2:
            send_big[s, h, g] = value
        else:
            send_small[s, h] = value
        owner, copy = sum_copy(s, h, g)

        @pl.when(owner == me)
        def _():
            if g < 2:
                recv_big[g, me] = value
            else:
                recv_small[me] = value

        @pl.when(owner != me)
        def _():
            copy.start()

    def product(values, k, part=(0, DEPTH)):
        high, low = halves(values)
        count = values.shape[0]
        both = by_rows(jnp.concatenate([high, low], axis=0), ints_high[k, :, pl.ds(*part)])
        rest = by_rows(high, ints_low[k, :, pl.ds(*part)])
        return both[:count] + (both[count:] + rest)

    even[...] = jnp.zeros_like(even)
    odd[...] = jnp.zeros_like(odd)

    def split_block(b, carry):
        ints_copy(b).wait()

        def split(t, inner):
            part = pl.ds(pl.multiple_of(b * BLOCK + t * 16, 16), 16)
            for k in range(slices):
                length = min(DEPTH, pairs - k * DEPTH)
                high, low = halves(wide_ints[part, k * DEPTH:k * DEPTH + length])
                ints_high[k, part, :length] = high
                ints_low[k, part, :length] = low
                if length < DEPTH:
                    nothing = jnp.zeros((16, DEPTH - length), BF16)
                    ints_high[k, part, length:] = nothing
                    ints_low[k, part, length:] = nothing
            return inner

        lax.fori_loop(0, BLOCK // 16, split, 0)

        @pl.when(lax.rem(b, 2) == 1)
        def _():
            far_copy(AHEAD + lax.div(b, 2)).start()

        return carry

    lax.fori_loop(0, blocks, split_block, 0)
    twin_copy.wait_recv()

    early = AHEAD + blocks // 2
    issued = early + slices

    def near_step(j, carry):
        for p, total in ((0, even), (1, odd)):
            k = 2 * j + p
            parts = [
                mine[3 * j + 1 + p], mine[light + k], twin[3 * j + 1 + p], twin[light + k],
                mine[3 * j], twin[3 * j],
            ]
            total[...] += product(jnp.concatenate(parts, axis=0), k)
        for p in range(2):
            far_copy(early + 2 * j + p).start()
        return carry

    lax.fori_loop(0, slices // 2, near_step, 0)
    for s in range(2):
        for h in range(2):
            for g in range(2):
                at = 4 * third * s + 2 * third * g + third * h
                emit(s, h, g, even[at:at + third] + odd[at:at + third])
            at = 8 * third + 4 * small * s + small * h
            emit(s, h, 2, even[at:at + small] + odd[at + 2 * small:at + 3 * small])

    def arrive(i):
        far_copy(i).wait_recv()
        pass_copy(i).start()

        @pl.when((i >= issued - AHEAD) & (i < steps - 1 - AHEAD))
        def _():
            far_copy(i + AHEAD).start()

        @pl.when(i == steps - 1 - AHEAD)
        def _():
            for piece in range(2):
                far_copy(steps - 1, piece).start()

    def arrive_last(piece):
        far_copy(steps - 1, piece).wait_recv()
        pass_copy(steps - 1, piece).start()

    far_even[...] = jnp.zeros_like(far_even)
    far_odd[...] = jnp.zeros_like(far_odd)
    arrive(0)
    arrive(1)

    def far_step(j, carry):
        arrive(3 * j + 2)
        pass_copy(3 * j).wait_recv()
        pass_copy(3 * j + 1).wait_recv()
        parts = [far[3 * j + 1], far_twin[3 * j + 1], far[3 * j], far_twin[3 * j]]
        far_even[...] += product(jnp.concatenate(parts, axis=0), 2 * j)
        arrive(3 * j + 3)

        @pl.when(j < slices // 2 - 1)
        def _():
            arrive(3 * j + 4)

        pass_copy(3 * j + 2).wait_recv()
        parts = [far[3 * j + 2], far_twin[3 * j + 2], far[3 * j], far_twin[3 * j]]
        far_odd[...] += product(jnp.concatenate(parts, axis=0), 2 * j + 1)
        return carry

    lax.fori_loop(0, slices // 2, far_step, 0)
    for s in range(2):
        for h in range(2):
            at = 2 * third * s + third * h
            emit(2 + s, h, 0, far_even[at:at + third] + far_odd[at:at + third])
            at = 4 * third + 4 * small * s + small * h
            emit(2 + s, h, 2, far_even[at:at + small] + far_odd[at + 2 * small:at + 3 * small])

    def light_product(k):
        pass_copy(light + k).wait_recv()
        group_sum[...] += product(
            jnp.concatenate([far[light + k], far_twin[light + k]], axis=0), k
        )

    def light_step(k, carry):
        arrive(light + k + 1)
        light_product(k)
        return carry

    group_sum[...] = jnp.zeros_like(group_sum)
    lax.fori_loop(0, slices - 2, light_step, 0)
    arrive_last(0)
    light_product(slices - 2)
    arrive_last(1)
    for piece in range(2):
        pass_copy(steps - 1, piece).wait_recv()
        part = pl.ds(*last_part[piece])
        group_sum[...] += product(
            jnp.concatenate([far[steps - 1, :, part], far_twin[steps - 1, :, part]], axis=0),
            slices - 1, last_part[piece],
        )
    for s in range(2):
        for h in range(2):
            at = 2 * third * s + third * h
            emit(2 + s, h, 1, group_sum[at:at + third])

    def drain(i, carry):
        far_copy(i).wait_send()
        pass_copy(i).wait_send()
        return carry

    lax.fori_loop(0, steps - 1, drain, 0)
    for piece in range(2):
        far_copy(steps - 1, piece).wait_send()
        pass_copy(steps - 1, piece).wait_send()
    twin_copy.wait_send()

    for g in (0, 2, 1):
        for source in range(wides):
            @pl.when(me != source)
            def _():
                dst = recv_big.at[g, source] if g < 2 else recv_small.at[source]
                pltpu.make_async_remote_copy(
                    src_ref=dst, dst_ref=dst,
                    send_sem=sum_send.at[0, 0, g], recv_sem=sum_recv.at[g, source],
                    device_id=(source, narrow), device_id_type=MESH,
                ).wait_recv()
        held = recv_big.at[g] if g < 2 else recv_small
        total = held[0]
        for source in range(1, wides):
            total = total + held[source]
        part = pl.ds(g * third, total.shape[0])
        result[part, :] = total / bottom[part, :]

    out_copy = pltpu.make_async_copy(result, out, out_sem)
    out_copy.start()
    for s in range(4):
        for h in range(2):
            for g in range(3):
                owner, copy = sum_copy(s, h, g)

                @pl.when(owner != me)
                def _():
                    copy.wait_send()
    out_copy.wait()


def fused_step(wides, amplitudes, integrals, occupied, virtual_rows, virtual_cols):
    rows, pairs = amplitudes.shape
    cols = integrals.shape[1]
    owner_rows = rows // 2
    third = 2 * owner_rows // 5
    small = owner_rows - 2 * third
    slices = 2 * pl.cdiv(pairs, 2 * DEPTH)
    steps = 2 * slices + slices // 2
    chunks = pltpu.VMEM((steps, 2 * third, DEPTH), F32)
    near_rows = 8 * third + 8 * small
    far_rows = 4 * third
    dma = pltpu.SemaphoreType.DMA
    any_spec = pl.BlockSpec(memory_space=pl.ANY)
    hbm_spec = pl.BlockSpec(memory_space=pltpu.HBM)
    return pl.pallas_call(
        functools.partial(cycle_kernel, wides),
        out_shape=jax.ShapeDtypeStruct((owner_rows, cols), F32),
        in_specs=[hbm_spec] * 5,
        out_specs=any_spec,
        scratch_shapes=[
            pltpu.VMEM((rows, pairs), F32),
            chunks, chunks, chunks, chunks,
            pltpu.VMEM((cols, pairs), F32),
            pltpu.VMEM((slices, cols, DEPTH), BF16),
            pltpu.VMEM((slices, cols, DEPTH), BF16),
            pltpu.VMEM((near_rows, cols), F32),
            pltpu.VMEM((near_rows, cols), F32),
            pltpu.VMEM((far_rows, cols), F32),
            pltpu.VMEM((far_rows + 8 * small, cols), F32),
            pltpu.VMEM((far_rows + 8 * small, cols), F32),
            pltpu.VMEM((4, 2, 2, third, cols), F32),
            pltpu.VMEM((4, 2, small, cols), F32),
            pltpu.VMEM((2, wides, third, cols), F32),
            pltpu.VMEM((wides, small, cols), F32),
            dma, dma((cols // BLOCK,)), dma((steps + 1,)), dma((steps + 1,)),
            dma((steps + 1,)), dma((steps + 1,)),
            dma, dma, dma((4, 2, 3)), dma((3, wides)),
            pltpu.VMEM(occupied.shape, F32),
            pltpu.SMEM(occupied.shape, F32),
            pltpu.SMEM(virtual_rows.shape, F32),
            pltpu.SMEM(virtual_cols.shape, F32),
            pltpu.VMEM((1, cols), F32),
            pltpu.VMEM((owner_rows, cols), F32),
            dma((4,)),
            pltpu.VMEM((owner_rows, cols), F32), dma,
        ],
        compiler_params=pltpu.CompilerParams(
            collective_id=0, has_side_effects=True, vmem_limit_bytes=52 * 1024 * 1024
        ),
        cost_estimate=pl.CostEstimate(
            flops=6 * 4 * rows * pairs * cols,
            bytes_accessed=4 * pairs * (rows + cols),
            transcendentals=0,
        ),
    )(amplitudes, integrals.T, occupied, virtual_rows, virtual_cols)


def plain_term(amplitudes, integrals):
    partial_term = jnp.dot(
        lax.all_gather(amplitudes, "narrow", axis=0, tiled=True),
        integrals,
        precision=lax.Precision.HIGHEST,
        preferred_element_type=F32,
    )
    return lax.psum_scatter(partial_term, "wide", scatter_dimension=0, tiled=True)


def per_device(wides, narrows, amplitudes, integrals, occupied_energy, virtual_energy_rows, virtual_energy_cols):
    rows = amplitudes.shape[0]
    if narrows == 4 and wides == 8 and rows % 20 == 0 and integrals.shape[1] % BLOCK == 0:
        return fused_step(
            wides, amplitudes, integrals,
            occupied_energy, virtual_energy_rows, virtual_energy_cols,
        )
    cycle_term = plain_term(amplitudes, integrals)
    row_count = cycle_term.shape[0]
    col_count = cycle_term.shape[1]
    row_first = lax.axis_index("wide") * row_count
    col_first = lax.axis_index("narrow") * col_count
    row_energy = (occupied_energy[None, :] - virtual_energy_rows[:, None]).reshape(-1)
    col_energy = (occupied_energy[None, :] - virtual_energy_cols[:, None]).reshape(-1)
    row_part = lax.dynamic_slice_in_dim(row_energy, row_first, row_count)
    col_part = lax.dynamic_slice_in_dim(col_energy, col_first, col_count)
    denominator = row_part[:, None] + col_part[None, :]
    return cycle_term / denominator


def solution(mesh):
    in_specs = (P("narrow", "wide"), P("wide", "narrow"), P(), P(), P())
    out_specs = P("wide", "narrow")
    body = functools.partial(per_device, mesh.shape["wide"], mesh.shape["narrow"])
    return jax.shard_map(
        body, mesh=mesh, in_specs=in_specs, out_specs=out_specs, check_vma=False
    )
```

```python
import functools

import jax
import jax.numpy as jnp
from jax import lax
from jax.experimental import pallas as pl
from jax.experimental.pallas import tpu as pltpu
from jax.sharding import PartitionSpec as P

MESH = pl.DeviceIdType.MESH
F32 = jnp.float32
BF16 = jnp.bfloat16
DEPTH = 1152
AHEAD = 4
BLOCK = 80


def halves(values):
    high = values.astype(BF16)
    return high, (values - high.astype(F32)).astype(BF16)


def by_rows(left, right):
    return lax.dot_general(
        left, right, (((1,), (1,)), ((), ())), preferred_element_type=F32
    )


def cycle_kernel(
    wides, occupied_count, rows_count, amp, ints, cells, out,
    own, mine, twin, far, far_twin, wide_ints, ints_high, ints_low,
    even, odd, group_sum, far_even, far_odd,
    send_big, send_small, recv_big, recv_small,
    own_sem, ints_sem, far_send, far_recv, pass_send, pass_recv, twin_send, twin_recv,
    sum_send, sum_recv,
    col_part, bottom, result, out_sem,
):
    rows, pairs = amp.shape
    owner_rows = rows // 2
    third = 2 * owner_rows // 5
    small = owner_rows - 2 * third
    steps = mine.shape[0]
    slices = ints_high.shape[0]
    last_length = pl.cdiv(pairs - (slices - 1) * DEPTH, 128) * 128
    first_length = pl.cdiv(last_length, 256) * 128
    light = 3 * slices // 2
    me = lax.axis_index("wide")
    narrow = lax.axis_index("narrow")
    across = lax.div(narrow, 2)
    core = lax.rem(narrow, 2)
    sibling = narrow + 1 - 2 * core
    neighbour = narrow + 2 - 4 * across
    diagonal = sibling + 2 - 4 * across
    shards = (narrow, sibling, neighbour, diagonal)

    own_copy = pltpu.make_async_copy(amp, own, own_sem)
    own_copy.start()

    def ints_copy(b):
        part = pl.ds(b * BLOCK, BLOCK)
        return pltpu.make_async_copy(ints.at[part], wide_ints.at[part], ints_sem.at[b])

    blocks = ints.shape[0] // BLOCK

    barrier = pltpu.get_barrier_semaphore()
    for other in (sibling, neighbour):
        pl.semaphore_signal(barrier, inc=1, device_id=(me, other), device_id_type=MESH)
    for hop in range(1, wides):
        pl.semaphore_signal(
            barrier, inc=1, device_id=(lax.rem(me + hop, wides), narrow), device_id_type=MESH
        )
    pl.semaphore_wait(barrier, wides + 1)

    last_part = [(0, first_length), (first_length, last_length - first_length)]

    def chunk(buffer, i, piece):
        if piece is None:
            return buffer.at[i]
        return buffer.at[i, :, pl.ds(*last_part[piece])]

    def far_copy(i, piece=None):
        at = i + (piece or 0)
        return pltpu.make_async_remote_copy(
            src_ref=chunk(mine, i, piece), dst_ref=chunk(far, i, piece),
            send_sem=far_send.at[at], recv_sem=far_recv.at[at],
            device_id=(me, neighbour), device_id_type=MESH,
        )

    def pass_copy(i, piece=None):
        at = i + (piece or 0)
        return pltpu.make_async_remote_copy(
            src_ref=chunk(far, i, piece), dst_ref=chunk(far_twin, i, piece),
            send_sem=pass_send.at[at], recv_sem=pass_recv.at[at],
            device_id=(me, sibling), device_id_type=MESH,
        )

    twin_copy = pltpu.make_async_remote_copy(
        src_ref=mine, dst_ref=twin, send_sem=twin_send, recv_sem=twin_recv,
        device_id=(me, sibling), device_id_type=MESH,
    )

    def pack(i, at, first, count, k):
        length = min(DEPTH, pairs - k * DEPTH)
        mine[i, at:at + count, :length] = own[first:first + count, k * DEPTH:k * DEPTH + length]
        if length < DEPTH:
            mine[i, at:at + count, length:] = jnp.zeros((count, DEPTH - length), F32)

    own_copy.wait()
    for j in range(slices // 2):
        for p in range(2):
            pack(3 * j, 2 * small * p, 2 * third, small, 2 * j + p)
            pack(3 * j, 2 * small * p + small, owner_rows + 2 * third, small, 2 * j + p)
        for p in range(2):
            i = 3 * j + 1 + p
            pack(i, 0, 0, third, 2 * j + p)
            pack(i, third, owner_rows, third, 2 * j + p)
        if j == 0:
            for i in range(AHEAD // 2):
                far_copy(i).start()
            for b in range(blocks):
                ints_copy(b).start()
    for k in range(slices):
        pack(light + k, 0, third, third, k)
        pack(light + k, third, owner_rows + third, third, k)
    twin_copy.start()
    for i in range(AHEAD // 2, AHEAD):
        far_copy(i).start()

    cols_at = occupied_count + rows_count
    lane = lax.broadcasted_iota(jnp.int32, (1, occupied_count), 1)
    occupied_lanes = jnp.zeros((1, occupied_count), F32)
    for i in range(occupied_count):
        occupied_lanes = jnp.where(lane == i, cells[i], occupied_lanes)
    for b in range(ints.shape[0] // occupied_count):
        col_part[:, b * occupied_count:(b + 1) * occupied_count] = (
            occupied_lanes
            - cells[cols_at + narrow * (ints.shape[0] // occupied_count) + b]
        )
    first = me * owner_rows
    virtual = cells[occupied_count + lax.div(first, occupied_count)]
    for r in range(owner_rows):
        row_part = cells[lax.rem(first, occupied_count) + r] - virtual
        bottom[r:r + 1, :] = row_part + col_part[...]

    def sum_copy(s, h, g):
        owner = 2 * shards[s] + h
        src = send_big.at[s, h, g] if g < 2 else send_small.at[s, h]
        dst = recv_big.at[g, me] if g < 2 else recv_small.at[me]
        copy = pltpu.make_async_remote_copy(
            src_ref=src, dst_ref=dst,
            send_sem=sum_send.at[s, h, g], recv_sem=sum_recv.at[g, me],
            device_id=(owner, narrow), device_id_type=MESH,
        )
        return owner, copy

    def emit(s, h, g, value):
        if g < 2:
            send_big[s, h, g] = value
        else:
            send_small[s, h] = value
        owner, copy = sum_copy(s, h, g)

        @pl.when(owner == me)
        def _():
            if g < 2:
                recv_big[g, me] = value
            else:
                recv_small[me] = value

        @pl.when(owner != me)
        def _():
            copy.start()

    def product(values, k, part=(0, DEPTH)):
        high, low = halves(values)
        count = values.shape[0]
        both = by_rows(jnp.concatenate([high, low], axis=0), ints_high[k, :, pl.ds(*part)])
        rest = by_rows(high, ints_low[k, :, pl.ds(*part)])
        return both[:count] + (both[count:] + rest)

    even[...] = jnp.zeros_like(even)
    odd[...] = jnp.zeros_like(odd)

    def split_block(b, carry):
        ints_copy(b).wait()

        def split(t, inner):
            part = pl.ds(pl.multiple_of(b * BLOCK + t * 16, 16), 16)
            for k in range(slices):
                length = min(DEPTH, pairs - k * DEPTH)
                high, low = halves(wide_ints[part, k * DEPTH:k * DEPTH + length])
                ints_high[k, part, :length] = high
                ints_low[k, part, :length] = low
                if length < DEPTH:
                    nothing = jnp.zeros((16, DEPTH - length), BF16)
                    ints_high[k, part, length:] = nothing
                    ints_low[k, part, length:] = nothing
            return inner

        lax.fori_loop(0, BLOCK // 16, split, 0)

        @pl.when(lax.rem(b, 2) == 1)
        def _():
            far_copy(AHEAD + lax.div(b, 2)).start()

        return carry

    lax.fori_loop(0, blocks, split_block, 0)
    twin_copy.wait_recv()

    early = AHEAD + blocks // 2
    issued = early + slices

    def near_step(j, carry):
        for p, total in ((0, even), (1, odd)):
            k = 2 * j + p
            parts = [
                mine[3 * j + 1 + p], mine[light + k], twin[3 * j + 1 + p], twin[light + k],
                mine[3 * j], twin[3 * j],
            ]
            total[...] += product(jnp.concatenate(parts, axis=0), k)
        for p in range(2):
            far_copy(early + 2 * j + p).start()
        return carry

    lax.fori_loop(0, slices // 2, near_step, 0)
    for s in range(2):
        for h in range(2):
            for g in range(2):
                at = 4 * third * s + 2 * third * g + third * h
                emit(s, h, g, even[at:at + third] + odd[at:at + third])
            at = 8 * third + 4 * small * s + small * h
            emit(s, h, 2, even[at:at + small] + odd[at + 2 * small:at + 3 * small])

    def arrive(i):
        far_copy(i).wait_recv()
        pass_copy(i).start()

        @pl.when((i >= issued - AHEAD) & (i < steps - 1 - AHEAD))
        def _():
            far_copy(i + AHEAD).start()

        @pl.when(i == steps - 1 - AHEAD)
        def _():
            for piece in range(2):
                far_copy(steps - 1, piece).start()

    def arrive_last(piece):
        far_copy(steps - 1, piece).wait_recv()
        pass_copy(steps - 1, piece).start()

    far_even[...] = jnp.zeros_like(far_even)
    far_odd[...] = jnp.zeros_like(far_odd)
    arrive(0)
    arrive(1)

    def far_step(j, carry):
        arrive(3 * j + 2)
        pass_copy(3 * j).wait_recv()
        pass_copy(3 * j + 1).wait_recv()
        parts = [far[3 * j + 1], far_twin[3 * j + 1], far[3 * j], far_twin[3 * j]]
        far_even[...] += product(jnp.concatenate(parts, axis=0), 2 * j)
        arrive(3 * j + 3)

        @pl.when(j < slices // 2 - 1)
        def _():
            arrive(3 * j + 4)

        pass_copy(3 * j + 2).wait_recv()
        parts = [far[3 * j + 2], far_twin[3 * j + 2], far[3 * j], far_twin[3 * j]]
        far_odd[...] += product(jnp.concatenate(parts, axis=0), 2 * j + 1)
        return carry

    lax.fori_loop(0, slices // 2, far_step, 0)
    for s in range(2):
        for h in range(2):
            at = 2 * third * s + third * h
            emit(2 + s, h, 0, far_even[at:at + third] + far_odd[at:at + third])
            at = 4 * third + 4 * small * s + small * h
            emit(2 + s, h, 2, far_even[at:at + small] + far_odd[at + 2 * small:at + 3 * small])

    def light_product(k):
        pass_copy(light + k).wait_recv()
        group_sum[...] += product(
            jnp.concatenate([far[light + k], far_twin[light + k]], axis=0), k
        )

    def light_step(k, carry):
        arrive(light + k + 1)
        light_product(k)
        return carry

    group_sum[...] = jnp.zeros_like(group_sum)
    lax.fori_loop(0, slices - 2, light_step, 0)
    arrive_last(0)
    light_product(slices - 2)
    arrive_last(1)
    for piece in range(2):
        pass_copy(steps - 1, piece).wait_recv()
        part = pl.ds(*last_part[piece])
        group_sum[...] += product(
            jnp.concatenate([far[steps - 1, :, part], far_twin[steps - 1, :, part]], axis=0),
            slices - 1, last_part[piece],
        )
    for s in range(2):
        for h in range(2):
            at = 2 * third * s + third * h
            emit(2 + s, h, 1, group_sum[at:at + third])

    def drain(i, carry):
        far_copy(i).wait_send()
        pass_copy(i).wait_send()
        return carry

    lax.fori_loop(0, steps - 1, drain, 0)
    for piece in range(2):
        far_copy(steps - 1, piece).wait_send()
        pass_copy(steps - 1, piece).wait_send()
    twin_copy.wait_send()

    for g in (0, 2, 1):
        for source in range(wides):
            @pl.when(me != source)
            def _():
                dst = recv_big.at[g, source] if g < 2 else recv_small.at[source]
                pltpu.make_async_remote_copy(
                    src_ref=dst, dst_ref=dst,
                    send_sem=sum_send.at[0, 0, g], recv_sem=sum_recv.at[g, source],
                    device_id=(source, narrow), device_id_type=MESH,
                ).wait_recv()
        held = recv_big.at[g] if g < 2 else recv_small
        total = held[0]
        for source in range(1, wides):
            total = total + held[source]
        part = pl.ds(g * third, total.shape[0])
        result[part, :] = total / bottom[part, :]

    out_copy = pltpu.make_async_copy(result, out, out_sem)
    out_copy.start()
    for s in range(4):
        for h in range(2):
            for g in range(3):
                owner, copy = sum_copy(s, h, g)

                @pl.when(owner != me)
                def _():
                    copy.wait_send()
    out_copy.wait()


def fused_step(wides, amplitudes, integrals, occupied, virtual_rows, virtual_cols):
    rows, pairs = amplitudes.shape
    cols = integrals.shape[1]
    owner_rows = rows // 2
    third = 2 * owner_rows // 5
    small = owner_rows - 2 * third
    slices = 2 * pl.cdiv(pairs, 2 * DEPTH)
    steps = 2 * slices + slices // 2
    chunks = pltpu.VMEM((steps, 2 * third, DEPTH), F32)
    near_rows = 8 * third + 8 * small
    far_rows = 4 * third
    dma = pltpu.SemaphoreType.DMA
    any_spec = pl.BlockSpec(memory_space=pl.ANY)
    cell_spec = pl.BlockSpec(memory_space=pltpu.SMEM)
    return pl.pallas_call(
        functools.partial(cycle_kernel, wides, occupied.shape[0], virtual_rows.shape[0]),
        out_shape=jax.ShapeDtypeStruct((owner_rows, cols), F32),
        in_specs=[any_spec, any_spec, cell_spec],
        out_specs=any_spec,
        scratch_shapes=[
            pltpu.VMEM((rows, pairs), F32),
            chunks, chunks, chunks, chunks,
            pltpu.VMEM((cols, pairs), F32),
            pltpu.VMEM((slices, cols, DEPTH), BF16),
            pltpu.VMEM((slices, cols, DEPTH), BF16),
            pltpu.VMEM((near_rows, cols), F32),
            pltpu.VMEM((near_rows, cols), F32),
            pltpu.VMEM((far_rows, cols), F32),
            pltpu.VMEM((far_rows + 8 * small, cols), F32),
            pltpu.VMEM((far_rows + 8 * small, cols), F32),
            pltpu.VMEM((4, 2, 2, third, cols), F32),
            pltpu.VMEM((4, 2, small, cols), F32),
            pltpu.VMEM((2, wides, third, cols), F32),
            pltpu.VMEM((wides, small, cols), F32),
            dma, dma((cols // BLOCK,)), dma((steps + 1,)), dma((steps + 1,)),
            dma((steps + 1,)), dma((steps + 1,)),
            dma, dma, dma((4, 2, 3)), dma((3, wides)),
            pltpu.VMEM((1, cols), F32),
            pltpu.VMEM((owner_rows, cols), F32),
            pltpu.VMEM((owner_rows, cols), F32), dma,
        ],
        compiler_params=pltpu.CompilerParams(
            collective_id=0, has_side_effects=True, vmem_limit_bytes=52 * 1024 * 1024
        ),
        cost_estimate=pl.CostEstimate(
            flops=6 * 4 * rows * pairs * cols,
            bytes_accessed=4 * pairs * (rows + cols),
            transcendentals=0,
        ),
    )(amplitudes, integrals.T, jnp.concatenate([occupied, virtual_rows, virtual_cols]))


def plain_term(amplitudes, integrals):
    partial_term = jnp.dot(
        lax.all_gather(amplitudes, "narrow", axis=0, tiled=True),
        integrals,
        precision=lax.Precision.HIGHEST,
        preferred_element_type=F32,
    )
    return lax.psum_scatter(partial_term, "wide", scatter_dimension=0, tiled=True)


def per_device(wides, narrows, amplitudes, integrals, occupied_energy, virtual_energy_rows, virtual_energy_cols):
    rows = amplitudes.shape[0]
    if narrows == 4 and wides == 8 and rows % 20 == 0 and integrals.shape[1] % BLOCK == 0:
        return fused_step(
            wides, amplitudes, integrals,
            occupied_energy, virtual_energy_rows, virtual_energy_cols,
        )
    cycle_term = plain_term(amplitudes, integrals)
    row_count = cycle_term.shape[0]
    col_count = cycle_term.shape[1]
    row_first = lax.axis_index("wide") * row_count
    col_first = lax.axis_index("narrow") * col_count
    row_energy = (occupied_energy[None, :] - virtual_energy_rows[:, None]).reshape(-1)
    col_energy = (occupied_energy[None, :] - virtual_energy_cols[:, None]).reshape(-1)
    row_part = lax.dynamic_slice_in_dim(row_energy, row_first, row_count)
    col_part = lax.dynamic_slice_in_dim(col_energy, col_first, col_count)
    denominator = row_part[:, None] + col_part[None, :]
    return cycle_term / denominator


def solution(mesh):
    in_specs = (P("narrow", "wide"), P("wide", "narrow"), P(), P(), P())
    out_specs = P("wide", "narrow")
    body = functools.partial(per_device, mesh.shape["wide"], mesh.shape["narrow"])
    return jax.shard_map(
        body, mesh=mesh, in_specs=in_specs, out_specs=out_specs, check_vma=False
    )
```
